256 devices in a mesh: dp: 32 (over z, y_hi, core), mp: 8 (over y_lo, x).
Axes of the slice: x: 4, y: 4 (y_hi: 2, y_lo: 2; y = y_hi * 2 + y_lo), z: 8, core: 2. Of those that a mesh axis runs over, the one named last changes fastest.
Arguments:
- activations: bfloat16 [8192, 8192], P('dp'), may hold values from -6 to 6
- out_grad: bfloat16 [8192, 28672], P('dp', 'mp'), may hold values from -8 to 8
- basis: bfloat16 [8192, 1024], P('dp'), may hold values from -0.0625 to 0.0625
- first_moment: float32 [28672, 1024], P(('mp', 'dp')), may hold values from -0.013258252 to 0.013258252
- second_moment: float32 [28672, 1024], P(('mp', 'dp')), may hold values from 1.2207032e-07 to 1.2207031e-06
Outputs:
- update: bfloat16 [8192, 28672], P('dp', 'mp')
- new_first: float32 [28672, 1024], P(('mp', 'dp'))
- new_second: float32 [28672, 1024], P(('mp', 'dp'))
The draws below stay inside these ranges and needn't reach their ends.
All inputs are finite; a program needn't handle non-finite values.
Results may differ from the reference program's by a relative error of at most 0.017.
Values may be sent and summed in bfloat16 or wider, within the bound.
No kernel may reach another device: no remote copies, remote signals or barrier semaphores. Data moves between devices by JAX's collectives and lax.ppermute only.
A program may use at most 128 MiB of HBM per device.

```python
import math
import jax
import jax.numpy as jnp
from jax import lax

D = 8192
FF = 28672
R = 1024
STEP = 10
TOK_DEV = 256
TOKENS = 8192
N_DP = 32


def raised(values, rng, source, target, shards_of, factor):
    def block_of(dim):
        return (jnp.arange(values.shape[dim]) // (values.shape[dim] // shards_of)).reshape((-1,) + (1,) * (values.ndim - 1 - dim))

    one_side = jax.random.permutation(rng, shards_of)[block_of(target)]
    other_side = (block_of(target) + shards_of // 2) % shards_of
    return jnp.where((block_of(source) == one_side) | (block_of(source) == other_side), factor * values, values)


def levels(key, extent, pieces, low, largest):
    gain, own = 1.0, jax.random.fold_in(key, 6)
    for axis_at, blocks in pieces:
        steps = jnp.exp(jax.random.uniform(jax.random.fold_in(own, axis_at), (blocks,), jnp.float32, low / len(pieces), largest / len(pieces)))
        gain = gain * jnp.repeat(steps, extent[axis_at] // blocks).reshape([-1 if axis == axis_at else 1 for axis in range(len(extent))])
    return gain


def bell_draw(own_key, dims, width, bound, split=(), held_as=jnp.bfloat16):
    array = width * jax.random.normal(own_key, dims, jnp.float32)
    if split:
        array = array * levels(own_key, dims, split, -0.22, 0.18)
    return jnp.clip(array, -bound, bound).astype(held_as)


def heavy_noise(key, extent, scale, limit, cuts, heavy, held_as=jnp.bfloat16):
    drawn = scale * jax.random.normal(key, extent, jnp.float32)
    if cuts:
        drawn = drawn * levels(key, extent, cuts, -0.22, 0.18)
    return jnp.clip(raised(drawn, jax.random.fold_in(key, 3), *heavy), -limit, limit).astype(held_as)


def setup_inputs(seed: int = 0) -> dict:
    splits = jax.random.split(jax.random.key(seed), 6)
    activations = bell_draw(splits[0], (TOKENS, D), 1.0, 6.0, ((0, 32),))
    out_grad = heavy_noise(splits[1], (TOKENS, FF), 1.0, 8.0, ((0, 32), (1, 8)), (0, 1, 32, 2.75))
    basis = bell_draw(splits[2], (D, R), D ** -0.5, 0.0625, ((0, 32),))
    first_moment = bell_draw(splits[3], (FF, R), (0.2 * TOKENS ** -0.5), 0.013258252, ((0, 256),), jnp.float32)
    second_moment = jnp.clip(jnp.exp(math.log(1.220703097715159e-06) - 2.30258502 * jax.random.uniform(splits[4], (FF, R), jnp.float32) ** levels(splits[4], (FF, R), ((0, 256),), -0.2, 0.2)), 1.2207031829802872e-07, 1.220703097715159e-06)
    return {"activations": activations, "out_grad": out_grad, "basis": basis, "first_moment": first_moment, "second_moment": second_moment}


def reference(activations, out_grad, basis, first_moment, second_moment):
    act_blocks = activations.reshape(N_DP, TOK_DEV, D)
    grad_blocks = out_grad.reshape(N_DP, TOK_DEV, FF)

    def add_block(total, pair):
        act_block, grad_block = pair
        projected = jnp.dot(act_block, basis, preferred_element_type=jnp.float32).astype(jnp.bfloat16)
        partial_sum = lax.dot_general(grad_block, projected, (((0,), (0,)), ((), ())), preferred_element_type=jnp.float32)
        return (total + partial_sum.astype(jnp.bfloat16).astype(jnp.float32), None)
    total, _ = lax.scan(add_block, jnp.zeros((FF, R), jnp.float32), (act_blocks, grad_blocks))
    low_grad = total / TOKENS
    new_first = 0.9 * first_moment + 0.1 * low_grad
    new_second = 0.999 * second_moment + 0.001 * low_grad * low_grad
    correct_one = 1.0 - 0.9 ** STEP
    correct_two = 1.0 - 0.999 ** STEP
    normalized = (new_first / correct_one / (jnp.sqrt(new_second / correct_two) + 1e-08)).astype(jnp.bfloat16)
    basis_blocks = basis.reshape(N_DP, D // N_DP, R)

    def expand(block):
        return lax.dot_general(block, normalized, (((1,), (1,)), ((), ())), preferred_element_type=jnp.float32).astype(jnp.bfloat16)
    update = lax.map(expand, basis_blocks).reshape(D, FF)
    return (update, new_first, new_second)
```

```python
import jax
import jax.numpy as jnp
from jax import lax
from jax.sharding import Mesh, PartitionSpec as P

STEP = 10
AXES = {"z": 8, "yh": 2, "c": 2, "yl": 2, "x": 4}
DP = ("z", "yh", "c")
MP = ("yl", "x")


def shift(value, axis, by):
    n = AXES[axis]
    return lax.ppermute(value, axis, [(i, (i + by) % n) for i in range(n)])


def swap(value, axes):
    n = 2 ** len(axes)
    return lax.ppermute(value, axes, [(i, n - 1 - i) for i in range(n)])


def absolute(stacked, axis):
    n = AXES[axis]
    start = (n - lax.axis_index(axis)) % n
    return lax.dynamic_slice_in_dim(jnp.concatenate([stacked, stacked[:-1]]), start, n)


def ring_gather(block):
    half = block.shape[0] // 2
    up, down = [block], [block]
    for _ in range(3):
        up.append(shift(up[-1], "z", 1))
        down.append(shift(down[-1], "z", -1))
    far = jnp.concatenate([shift(up[3][:half], "z", 1), shift(down[3][half:], "z", -1)])
    return [block, down[1], down[2], down[3], far, up[3], up[2], up[1]]


def shards(activations, out_grad, basis, first_moment, second_moment):
    tok, width = activations.shape
    ff = out_grad.shape[1]
    rows, rank = basis.shape
    own = ff // 32
    cols = rank // 8
    z, yh, c = (lax.axis_index(a) for a in DP)
    mp = lax.axis_index(MP)

    grad = jnp.transpose(out_grad).reshape(8, 2, 2, own, tok)

    def part(a, b):
        return grad[:, (yh + a) % 2, (c + b) % 2]

    grads = [part(0, 0), swap(part(0, 1), ("c",)), swap(part(1, 0), ("yh",)), swap(part(1, 1), ("yh", "c"))]

    bases = jnp.stack([basis, swap(basis, ("yh",))])
    bases = jnp.stack([bases, swap(bases, ("c",))])

    mine = lax.dynamic_slice_in_dim(basis, mp * cols, cols, 1)
    pair = jnp.stack([mine, swap(mine, ("yh",))]).reshape(2 * rows, cols)
    column = jnp.stack(ring_gather(pair)).reshape(8, 2, rows, cols)
    column = jnp.stack([column, swap(column, ("c",))])
    column = jnp.transpose(absolute(column, "c"), (1, 2, 0, 3, 4))
    column = absolute(column, "z")
    column = jnp.transpose(absolute(jnp.transpose(column, (1, 0, 2, 3, 4)), "yh"), (1, 0, 2, 3, 4))
    projected = jnp.dot(
        activations, column.reshape(width, cols), preferred_element_type=jnp.float32
    ).astype(jnp.bfloat16)

    line = absolute(jnp.stack([projected] + [shift(projected, "x", -d) for d in (1, 2, 3)]), "x")
    near = absolute(jnp.stack([line, swap(line, ("yl",))]), "yl")
    far = absolute(jnp.stack([swap(line, ("yh",)), swap(line, ("yh", "yl"))]), "yl")
    tokens = jnp.stack([near, far])
    tokens = jnp.stack([tokens, swap(tokens, ("c",))])
    tokens = jnp.transpose(tokens, (1, 0, 4, 2, 3, 5)).reshape(4 * tok, rank)
    grads = jnp.concatenate(grads, 2)

    def partial(d):
        block = lax.dynamic_index_in_dim(grads, (z + d) % 8, 0, keepdims=False)
        return jnp.dot(block, tokens, preferred_element_type=jnp.float32)

    total = partial(0)
    for d in (4, 3, 5, 2, 6, 1, 7):
        total = total + shift(partial(d).astype(jnp.bfloat16), "z", d).astype(jnp.float32)
    low_grad = total / (tok * 32)
    new_first = 0.9 * first_moment + 0.1 * low_grad
    new_second = 0.999 * second_moment + 0.001 * low_grad * low_grad
    correct_one = 1.0 - 0.9**STEP
    correct_two = 1.0 - 0.999**STEP
    normalized = (new_first / correct_one / (jnp.sqrt(new_second / correct_two) + 1e-08)).astype(
        jnp.bfloat16
    )

    steps = jnp.stack(ring_gather(normalized)).reshape(8 * own, rank)

    def update_of(a, b):
        return lax.dot_general(
            steps, bases[b, a], (((1,), (1,)), ((), ())), preferred_element_type=jnp.float32
        ).astype(jnp.bfloat16).reshape(8, own, rows)

    made = jnp.stack([
        jnp.stack([update_of(0, 0), swap(update_of(0, 1), ("c",))]),
        jnp.stack([swap(update_of(1, 0), ("yh",)), swap(update_of(1, 1), ("yh", "c"))]),
    ])
    made = absolute(made, "yh")
    made = absolute(jnp.transpose(made, (1, 0, 2, 3, 4)), "c")
    made = absolute(jnp.transpose(made, (2, 1, 0, 3, 4)), "z")
    update = jnp.transpose(made.reshape(ff, rows))
    return (update, new_first, new_second)


def solution(mesh):
    grid = Mesh(mesh.devices.reshape(tuple(AXES.values())), tuple(AXES))
    placed = (P(DP, None), P(DP, MP), P(DP, None), P(MP + DP, None), P(MP + DP, None))
    return jax.shard_map(
        shards,
        mesh=grid,
        in_specs=placed,
        out_specs=(P(DP, MP), P(MP + DP, None), P(MP + DP, None)),
        check_vma=False,
    )
```

```python
import functools

import jax
import jax.numpy as jnp
from jax import lax
from jax.experimental import pallas as pl
from jax.experimental.pallas import tpu as pltpu
from jax.sharding import Mesh, PartitionSpec as P

STEP = 10
AXES = {"z": 8, "yh": 2, "c": 2, "yl": 2, "x": 4}
DP = ("z", "yh", "c")
MP = ("yl", "x")
F32 = jnp.float32
BF16 = jnp.bfloat16
TURN = (((1,), (1,)), ((), ()))
SUMS = (4, 3, 5, 2, 6, 1, 7, 0)
GROUPS = ((0, 1, 7), (2, 6), (3, 5), (4,))


def shift(value, axis, by):
    n = AXES[axis]
    return lax.ppermute(value, axis, [(i, (i + by) % n) for i in range(n)])


def swap(value, *axes):
    n = 2 ** len(axes)
    return lax.ppermute(value, axes, [(i, n - 1 - i) for i in range(n)])


def tie(*values):
    return lax.optimization_barrier(values)


def on_core(body, out, scalars, *arrays, flops=0, scratch=()):
    size = sum(a.size * a.dtype.itemsize for a in arrays)
    return pl.pallas_call(
        body,
        out_shape=out,
        in_specs=[pl.BlockSpec(memory_space=pltpu.SMEM)]
        + [pl.BlockSpec(memory_space=pltpu.VMEM)] * len(arrays),
        out_specs=jax.tree.map(lambda _: pl.BlockSpec(memory_space=pltpu.VMEM), out),
        scratch_shapes=list(scratch),
        cost_estimate=pl.CostEstimate(flops=flops, bytes_accessed=size, transcendentals=0),
        compiler_params=pltpu.CompilerParams(vmem_limit_bytes=40 * 2**20),
    )(scalars, *arrays)


def turn_grad(at, grad, near_own, near_other, far, scratch):
    z, yh, c = at[0], at[1], at[2]
    ff = grad.shape[1]
    own = ff // 32
    w = ff // 8
    for i in range(8):
        scratch[i * w : (i + 1) * w, :] = grad[:, i * w : (i + 1) * w].T
    for i, dz in enumerate(SUMS):
        for dyh, dc, out in ((0, 0, near_own), (0, 1, near_other), (1, 0, far.at[0]), (1, 1, far.at[1])):
            place = ((z + dz) % 8) * 4 + ((yh + dyh) % 2) * 2 + (c + dc) % 2
            start = pl.multiple_of(place * own, 16)
            out[i * own : (i + 1) * own] = scratch[pl.ds(start, own), :]


def project(steps, at, act, *refs):
    *held, total, last = refs
    z, yh, c = at[0], at[1], at[2]
    rows = held[0].shape[0] // 2

    def columns(dz, dyh, dc):
        place = (((z + dz) % 8) * 2 + (yh + dyh) % 2) * 2 + (c + dc) % 2
        return act[:, pl.ds(pl.multiple_of(place * rows, rows), rows)]

    result = jnp.zeros(total.shape, F32)
    for i, block in enumerate(held):
        for j, dz in enumerate(steps[i // 2]):
            for dyh in range(2):
                start = (2 * j + dyh) * rows
                result += jnp.dot(
                    columns(dz, dyh, i % 2), block[start : start + rows], preferred_element_type=F32
                )
    total[...] = result
    for i in range(4):
        last[:, i * rows : (i + 1) * rows] = columns(4, i % 2, i // 2)


def partial_sums(lo, at, g00, g10, g1, *refs):
    mats, refs = refs[:8], refs[8:]
    wide = mats[0].shape[1]
    if len(refs) == 1:
        (out,) = refs
    else:
        passed, out, kept = refs
        kept[...] = passed[...]
    rows = slice(lo, lo + out.shape[0])
    grads = (g00[rows], g10[rows], g1[0, rows], g1[1, rows])
    for n in range(2):
        result = jnp.dot(grads[0], mats[n][...], preferred_element_type=F32)
        for k in (1, 2, 3):
            result += jnp.dot(grads[k], mats[2 * k + n][...], preferred_element_type=F32)
        out[:, n * wide : (n + 1) * wide] = result.astype(out.dtype)


def adam(count, at, here, up, down, first, second, new_first, new_second, normalized):
    own, cols = first.shape[0], first.shape[1] // 8
    for i in range(8):
        place = at[3 + i]
        there = pl.ds(pl.multiple_of(place * cols, cols), cols)
        here_cols = slice(i * cols, (i + 1) * cols)
        total = here[-own:, here_cols]
        for part in (up, down):
            total += part[:, here_cols].astype(F32)
        low_grad = total / count
        one = 0.9 * first[:, there] + 0.1 * low_grad
        two = 0.999 * second[:, there] + 0.001 * low_grad * low_grad
        new_first[:, there] = one
        new_second[:, there] = two
        correct_one = 1.0 - 0.9**STEP
        correct_two = 1.0 - 0.999**STEP
        normalized[:, there] = (one / correct_one / (jnp.sqrt(two / correct_two) + 1e-08)).astype(BF16)


def place_update(at, *refs):
    near, far, others, (out, scratch) = refs[:4], refs[4:8], refs[8:10], refs[10:]
    z, yh, c = at[0], at[1], at[2]
    rows = out.shape[0]
    own = out.shape[1] // 32
    begin = [0, 0]
    for g, dzs in enumerate(GROUPS):
        for dyh, made in enumerate((near[g], far[g])):
            for i, dz in enumerate(dzs):
                for dc in range(2):
                    place = ((z + dz) % 8) * 4 + ((yh + dyh) % 2) * 2 + (c + dc) % 2
                    there = pl.ds(pl.multiple_of(place * own, 16), own)
                    if dc == 0:
                        scratch[there, :] = made[i * own : (i + 1) * own, :rows]
                    else:
                        start = begin[g // 2] + i * own
                        scratch[there, :] = others[g // 2][start : start + own]
            begin[g // 2] += len(dzs) * own
    w = out.shape[1] // 8
    for i in range(8):
        out[:, i * w : (i + 1) * w] = scratch[i * w : (i + 1) * w, :].T


def shards(activations, out_grad, basis, first_moment, second_moment):
    tok, width = activations.shape
    ff = out_grad.shape[1]
    rows, rank = basis.shape
    own = ff // 32
    cols = rank // 8
    half = own // 32 * 16
    z, yh, c, yl, x = (lax.axis_index(a) for a in AXES)
    by_distance = [((yl + i) % 2) * 4 + (x + j) % 4 for i in range(2) for j in range(4)]
    at = jnp.stack([z, yh, c] + by_distance).astype(jnp.int32)

    mine = lax.dynamic_slice_in_dim(basis, (yl * 4 + x) * cols, cols, 1)
    share = jax.ShapeDtypeStruct((8 * own, tok), BF16)
    near_own, near_other, far_grad = on_core(
        turn_grad,
        (share, share, jax.ShapeDtypeStruct((2, 8 * own, tok), BF16)),
        at, out_grad,
        scratch=[pltpu.VMEM((ff, tok), BF16)],
    )
    pair = jnp.concatenate([mine, swap(mine, "yh")])
    pair, near_own, near_other, far_grad = tie(pair, near_own, near_other, far_grad)
    far_grad = swap(far_grad, "yh")
    up, down = pair, pair
    held = [pair, swap(pair, "c")]
    for _ in range(3):
        up, down = shift(up, "z", 1), shift(down, "z", -1)
        both = jnp.concatenate([down, up])
        held += [both, swap(both, "c")]
    total, act = on_core(
        functools.partial(project, ((0,), (1, 7), (2, 6), (3, 5))),
        (jax.ShapeDtypeStruct((tok, cols), F32), jax.ShapeDtypeStruct((tok, 4 * rows), BF16)),
        at, activations, *held,
        flops=2 * tok * width * cols,
    )
    last = jnp.concatenate([shift(up[:rows], "z", 1), shift(down[rows:], "z", -1)])
    last = jnp.concatenate([last, swap(last, "c")])
    total, act = tie(total, act)
    projected = (total + jnp.dot(act, last, preferred_element_type=F32)).astype(BF16)
    projected, far_grad = tie(projected, far_grad)

    others = swap(jnp.stack([near_other, far_grad[1]]), "c")
    line = jnp.concatenate([projected] + [shift(projected, "x", -d) for d in (1, 2, 3)], 1)
    pieces = [line, swap(line, "yl"), swap(line, "yh"), swap(line, "yh", "yl")]
    grads = (near_own, far_grad[0], others, *pieces, *[swap(piece, "c") for piece in pieces])

    first = on_core(
        functools.partial(partial_sums, 0),
        jax.ShapeDtypeStruct((own, rank), BF16),
        at, *grads,
        flops=2 * own * 4 * tok * rank,
    )
    up, down = shift(first[:half], "z", 1), shift(first[half:], "z", -1)
    rest, basis = on_core(
        functools.partial(partial_sums, own),
        (jax.ShapeDtypeStruct((7 * own, rank), F32), jax.ShapeDtypeStruct(basis.shape, BF16)),
        at, *grads, basis,
        flops=2 * 7 * own * 4 * tok * rank,
    )
    bases = jnp.stack([basis, swap(basis, "yh")])
    bases = jnp.stack([bases, swap(bases, "c")], 1)
    near_bases, far_bases = bases[0].reshape(2 * rows, rank), bases[1].reshape(2 * rows, rank)
    three, five = rest[:own], rest[own : 2 * own]
    up = shift(jnp.concatenate([three[:half] + up, three[half:]]).astype(BF16), "z", 1)
    down = shift(jnp.concatenate([five[:half], five[half:] + down]).astype(BF16), "z", -1)
    for i in (2, 4):
        up = shift((rest[i * own : (i + 1) * own] + up).astype(BF16), "z", 1)
        down = shift((rest[(i + 1) * own : (i + 2) * own] + down).astype(BF16), "z", -1)
    state = jax.ShapeDtypeStruct((own, rank), F32)
    new_first, new_second, normalized = on_core(
        functools.partial(adam, tok * 32),
        (state, state, jax.ShapeDtypeStruct((own, rank), BF16)),
        at, rest, up, down, first_moment, second_moment,
    )

    up, down = shift(normalized, "z", 1), shift(normalized, "z", -1)
    blocks = [(normalized, down, up)]
    for _ in range(2):
        up, down = shift(up, "z", 1), shift(down, "z", -1)
        blocks.append((down, up))
    blocks.append((shift(up[:half], "z", 1), shift(down[half:], "z", -1)))
    near, far = [], []
    for held in blocks:
        held = jnp.concatenate(held)
        out = lax.dot_general(held, far_bases, TURN, preferred_element_type=F32).astype(BF16)
        far.append(swap(out, "yh"))
        near.append(lax.dot_general(held, near_bases, TURN, preferred_element_type=F32).astype(BF16))
    others = [
        swap(jnp.concatenate([part[g][:, rows:] for g in some for part in (near, far)]), "c")
        for some in ((0, 1), (2, 3))
    ]
    update = on_core(
        place_update,
        jax.ShapeDtypeStruct((rows, ff), BF16),
        at, *near, *far, *others,
        scratch=[pltpu.VMEM((ff, rows), BF16)],
    )
    return (update, new_first, new_second)


def solution(mesh):
    grid = Mesh(mesh.devices.reshape(tuple(AXES.values())), tuple(AXES))
    placed = (P(DP, None), P(DP, MP), P(DP, None), P(MP + DP, None), P(MP + DP, None))
    return jax.shard_map(
        shards,
        mesh=grid,
        in_specs=placed,
        out_specs=(P(DP, MP), P(MP + DP, None), P(MP + DP, None)),
        check_vma=False,
    )
```

```python
import functools

import jax
import jax.numpy as jnp
from jax import lax
from jax.experimental import pallas as pl
from jax.experimental.pallas import tpu as pltpu
from jax.sharding import Mesh, PartitionSpec as P

STEP = 10
AXES = {"z": 8, "yh": 2, "c": 2, "yl": 2, "x": 4}
DP = ("z", "yh", "c")
MP = ("yl", "x")
F32 = jnp.float32
BF16 = jnp.bfloat16
TURN = (((1,), (1,)), ((), ()))
SUMS = (4, 3, 5, 2, 6, 1, 7, 0)

GROUPS = ((0, 1, 7), (2, 6), (3, 5), (4,))


def shift(value, axis, by):
    n = AXES[axis]
    return lax.ppermute(value, axis, [(i, (i + by) % n) for i in range(n)])


def swap(value, *axes):
    n = 2 ** len(axes)
    return lax.ppermute(value, axes, [(i, n - 1 - i) for i in range(n)])


def tie(*values):
    return lax.optimization_barrier(values)


def on_core(body, out, scalars, *arrays, flops=0, scratch=()):
    size = sum(a.size * a.dtype.itemsize for a in arrays)
    return pl.pallas_call(
        body,
        out_shape=out,
        in_specs=[pl.BlockSpec(memory_space=pltpu.SMEM)]
        + [pl.BlockSpec(memory_space=pltpu.VMEM)] * len(arrays),
        out_specs=jax.tree.map(lambda _: pl.BlockSpec(memory_space=pltpu.VMEM), out),
        scratch_shapes=list(scratch),
        cost_estimate=pl.CostEstimate(flops=flops, bytes_accessed=size, transcendentals=0),
        compiler_params=pltpu.CompilerParams(vmem_limit_bytes=40 * 2**20),
    )(scalars, *arrays)


def turn_grad(at, grad, basis, near_own, near_other, far, scratch):
    z, yh, c = at[0], at[1], at[2]
    tok, ff = grad.shape
    own = ff // 32
    w = ff // 8
    for i in range(8):
        scratch[i * w : (i + 1) * w, :] = grad[:, i * w : (i + 1) * w].T
    for i, dz in enumerate(SUMS):
        for dyh, dc, out, first in ((0, 0, near_own, 0), (0, 1, near_other, 0), (1, 0, far, 0), (1, 1, far, 8 * own)):
            place = ((z + dz) % 8) * 4 + ((yh + dyh) % 2) * 2 + (c + dc) % 2
            start = pl.multiple_of(place * own, 16)
            out[first + i * own : first + (i + 1) * own] = scratch[pl.ds(start, own), :]
    rows = basis.shape[0]
    for i in range(basis.shape[1] // tok):
        for out, first in ((near_other, 8 * own), (far, 16 * own)):
            out[first + i * rows : first + (i + 1) * rows] = basis[:, i * tok : (i + 1) * tok]


def project(steps, at, act, *refs):
    *held, total, last = refs
    z, yh, c = at[0], at[1], at[2]
    rows = held[0].shape[0] // 2

    def columns(dz, dyh, dc):
        place = (((z + dz) % 8) * 2 + (yh + dyh) % 2) * 2 + (c + dc) % 2
        return act[:, pl.ds(pl.multiple_of(place * rows, rows), rows)]

    result = jnp.zeros(total.shape, F32)
    for i, block in enumerate(held):
        for j, dz in enumerate(steps[i // 2]):
            for dyh in range(2):
                start = (2 * j + dyh) * rows
                result += jnp.dot(
                    columns(dz, dyh, i % 2), block[start : start + rows], preferred_element_type=F32
                )
    total[...] = result
    for i in range(4):
        last[:, i * rows : (i + 1) * rows] = columns(4, i % 2, i // 2)


def partial_sums(lo, at, near_own, far, crossed, *refs):
    *mats, out = refs
    wide = mats[0].shape[1]
    rows = slice(lo, lo + out.shape[0])
    second = slice(crossed.shape[0] // 2 + lo, crossed.shape[0] // 2 + rows.stop)
    grads = (near_own[rows], far[rows], crossed[rows], crossed[second])
    for n in range(2):
        result = jnp.dot(grads[0], mats[n][...], preferred_element_type=F32)
        for k in (1, 2, 3):
            result += jnp.dot(grads[k], mats[2 * k + n][...], preferred_element_type=F32)
        out[:, n * wide : (n + 1) * wide] = result.astype(out.dtype)


def adam(count, at, here, up, down, first, second, new_first, new_second, normalized):
    own, cols = first.shape[0], first.shape[1] // 8
    for i in range(8):
        place = at[3 + i]
        there = pl.ds(pl.multiple_of(place * cols, cols), cols)
        here_cols = slice(i * cols, (i + 1) * cols)
        total = here[-own:, here_cols]
        for part in (up, down):
            total += part[:, here_cols].astype(F32)
        low_grad = total / count
        one = 0.9 * first[:, there] + 0.1 * low_grad
        two = 0.999 * second[:, there] + 0.001 * low_grad * low_grad
        new_first[:, there] = one
        new_second[:, there] = two
        correct_one = 1.0 - 0.9**STEP
        correct_two = 1.0 - 0.999**STEP
        normalized[:, there] = (one / correct_one / (jnp.sqrt(two / correct_two) + 1e-08)).astype(BF16)


def make(own, n, at, basis, far, crossed, *refs):
    blocks, (mine, other, beyond) = refs[:n], refs[-3:]
    rows, rank = basis.shape
    wide = far.shape[1]
    held = jnp.concatenate([block[...] for block in blocks])
    mine[...] = lax.dot_general(held, basis[...], TURN, preferred_element_type=F32).astype(BF16)
    for mat, first, out, cols in (
        (crossed, 8 * own, other, slice(0, rows)),
        (far, 16 * own, beyond, slice(0, rows)),
        (crossed, 8 * own + crossed.shape[0] // 2, beyond, slice(rows, 2 * rows)),
    ):
        result = jnp.zeros((held.shape[0], rows), F32)
        for i in range(rank // wide):
            part = mat[first + i * rows : first + (i + 1) * rows]
            result += lax.dot_general(
                held[:, i * wide : (i + 1) * wide], part, TURN, preferred_element_type=F32
            )
        out[:, cols] = result.astype(BF16)


def place_update(at, *refs):
    near, far, others, (out, scratch) = refs[:4], refs[4:8], refs[8:10], refs[10:]
    z, yh, c = at[0], at[1], at[2]
    rows = out.shape[0]
    own = out.shape[1] // 32
    begin = [0, 0]
    for g, dzs in enumerate(GROUPS):
        for dyh, made in enumerate((near[g], far[g])):
            for i, dz in enumerate(dzs):
                for dc in range(2):
                    place = ((z + dz) % 8) * 4 + ((yh + dyh) % 2) * 2 + (c + dc) % 2
                    there = pl.ds(pl.multiple_of(place * own, 16), own)
                    if dc == 0:
                        scratch[there, :] = made[i * own : (i + 1) * own, :rows]
                    else:
                        start = begin[g // 2] + i * own
                        scratch[there, :] = others[g // 2][start : start + own]
            begin[g // 2] += len(dzs) * own
    w = out.shape[1] // 8
    for i in range(8):
        out[:, i * w : (i + 1) * w] = scratch[i * w : (i + 1) * w, :].T


def shards(activations, out_grad, basis, first_moment, second_moment):
    tok, width = activations.shape
    ff = out_grad.shape[1]
    rows, rank = basis.shape
    own = ff // 32
    cols = rank // 8
    half = own // 32 * 16
    z, yh, c, yl, x = (lax.axis_index(a) for a in AXES)
    by_distance = [((yl + i) % 2) * 4 + (x + j) % 4 for i in range(2) for j in range(4)]
    at = jnp.stack([z, yh, c] + by_distance).astype(jnp.int32)

    mine = lax.dynamic_slice_in_dim(basis, (yl * 4 + x) * cols, cols, 1)
    near_own, near_other, far = on_core(
        turn_grad,
        tuple(
            jax.ShapeDtypeStruct((n, tok), BF16)
            for n in (8 * own, 8 * own + rows * rank // tok, 16 * own + rows * rank // tok)
        ),
        at, out_grad, basis,
        scratch=[pltpu.VMEM((ff, tok), BF16)],
    )
    pair = jnp.concatenate([mine, swap(mine, "yh")])
    pair, near_own, near_other, far = tie(pair, near_own, near_other, far)
    far = swap(far, "yh")
    up, down = pair, pair
    held = [pair, swap(pair, "c")]
    for _ in range(3):
        up, down = shift(up, "z", 1), shift(down, "z", -1)
        both = jnp.concatenate([down, up])
        held += [both, swap(both, "c")]
    total, act = on_core(
        functools.partial(project, ((0,), (1, 7), (2, 6), (3, 5))),
        (jax.ShapeDtypeStruct((tok, cols), F32), jax.ShapeDtypeStruct((tok, 4 * rows), BF16)),
        at, activations, *held,
        flops=2 * tok * width * cols,
    )
    last = jnp.concatenate([shift(up[:rows], "z", 1), shift(down[rows:], "z", -1)])
    last = jnp.concatenate([last, swap(last, "c")])
    total, act = tie(total, act)
    projected = (total + jnp.dot(act, last, preferred_element_type=F32)).astype(BF16)

    line = jnp.concatenate([projected] + [shift(projected, "x", -d) for d in (1, 2, 3)], 1)
    line, far = tie(line, far)
    crossed = swap(jnp.concatenate([near_other, far[8 * own :]]), "c")
    pieces = [line, swap(line, "yl"), swap(line, "yh"), swap(line, "yh", "yl")]
    others = (far, crossed)
    mats = (*pieces, *[swap(piece, "c") for piece in pieces])

    def partial(lo, hi, dtype):
        return on_core(
            functools.partial(partial_sums, lo * own),
            jax.ShapeDtypeStruct(((hi - lo) * own, rank), dtype),
            at, near_own, *others, *mats,
            flops=2 * (hi - lo) * own * 4 * tok * rank,
        )

    first = partial(0, 1, BF16)
    up, down = shift(first[:half], "z", 1), shift(first[half:], "z", -1)
    rest = partial(1, 8, F32)
    three, five = rest[:own], rest[own : 2 * own]
    up = shift(jnp.concatenate([three[:half] + up, three[half:]]).astype(BF16), "z", 1)
    down = shift(jnp.concatenate([five[:half], five[half:] + down]).astype(BF16), "z", -1)
    for i in (2, 4):
        up = shift((rest[i * own : (i + 1) * own] + up).astype(BF16), "z", 1)
        down = shift((rest[(i + 1) * own : (i + 2) * own] + down).astype(BF16), "z", -1)
    state = jax.ShapeDtypeStruct((own, rank), F32)
    new_first, new_second, normalized = on_core(
        functools.partial(adam, tok * 32),
        (state, state, jax.ShapeDtypeStruct((own, rank), BF16)),
        at, rest, up, down, first_moment, second_moment,
    )

    def made(blocks):
        n = sum(block.shape[0] for block in blocks)
        near, other, beyond = on_core(
            functools.partial(make, own, len(blocks)),
            [jax.ShapeDtypeStruct((n, i * rows), BF16) for i in (1, 1, 2)],
            at, basis, *others, *blocks,
            flops=2 * n * 4 * rows * rank,
        )
        return near, other, swap(beyond, "yh")

    up, down = shift(normalized, "z", 1), shift(normalized, "z", -1)
    groups = [made((normalized, down, up))]
    for _ in range(2):
        up, down = shift(up, "z", 1), shift(down, "z", -1)
        groups.append(made((down, up)))
    groups.append(made((shift(up[:half], "z", 1), shift(down[half:], "z", -1))))
    crossed = [
        swap(jnp.concatenate([p for g in some for p in (groups[g][1], groups[g][2][:, rows:])]), "c")
        for some in ((0, 1), (2, 3))
    ]
    update = on_core(
        place_update,
        jax.ShapeDtypeStruct((rows, ff), BF16),
        at, *[group[0] for group in groups], *[group[2] for group in groups], *crossed,
        scratch=[pltpu.VMEM((ff, rows), BF16)],
    )
    return (update, new_first, new_second)


def solution(mesh):
    grid = Mesh(mesh.devices.reshape(tuple(AXES.values())), tuple(AXES))
    placed = (P(DP, None), P(DP, MP), P(DP, None), P(MP + DP, None), P(MP + DP, None))
    return jax.shard_map(
        shards,
        mesh=grid,
        in_specs=placed,
        out_specs=(P(DP, MP), P(MP + DP, None), P(MP + DP, None)),
        check_vma=False,
    )
```

```python
import functools

import jax
import jax.numpy as jnp
from jax import lax
from jax.experimental import pallas as pl
from jax.experimental.pallas import tpu as pltpu
from jax.sharding import Mesh, PartitionSpec as P

STEP = 10
AXES = {"z": 8, "yh": 2, "c": 2, "yl": 2, "x": 4}
DP = ("z", "yh", "c")
MP = ("yl", "x")
F32 = jnp.float32
BF16 = jnp.bfloat16
TURN = (((1,), (1,)), ((), ()))
SUMS = (4, 3, 5, 2, 6, 1, 7, 0)

GROUPS = ((0, 1, 7), (2, 6), (3, 5), (4,))


def shift(value, axis, by):
    n = AXES[axis]
    return lax.ppermute(value, axis, [(i, (i + by) % n) for i in range(n)])


def swap(value, *axes):
    n = 2 ** len(axes)
    return lax.ppermute(value, axes, [(i, n - 1 - i) for i in range(n)])


def tie(*values):
    return lax.optimization_barrier(values)


def on_core(body, out, scalars, *arrays, flops=0, scratch=()):
    size = sum(a.size * a.dtype.itemsize for a in arrays)
    return pl.pallas_call(
        body,
        out_shape=out,
        in_specs=[pl.BlockSpec(memory_space=pltpu.SMEM)]
        + [pl.BlockSpec(memory_space=pltpu.VMEM)] * len(arrays),
        out_specs=jax.tree.map(lambda _: pl.BlockSpec(memory_space=pltpu.VMEM), out),
        scratch_shapes=list(scratch),
        cost_estimate=pl.CostEstimate(flops=flops, bytes_accessed=size, transcendentals=0),
        compiler_params=pltpu.CompilerParams(vmem_limit_bytes=40 * 2**20),
    )(scalars, *arrays)


def turn_grad(at, grad, basis, near_own, near_other, far, scratch):
    z, yh, c = at[0], at[1], at[2]
    tok, ff = grad.shape
    own = ff // 32
    w = ff // 8
    for i in range(8):
        scratch[i * w : (i + 1) * w, :] = grad[:, i * w : (i + 1) * w].T
    for i, dz in enumerate(SUMS):
        for dyh, dc, out, first in ((0, 0, near_own, 0), (0, 1, near_other, 0), (1, 0, far, 0), (1, 1, far, 8 * own)):
            place = ((z + dz) % 8) * 4 + ((yh + dyh) % 2) * 2 + (c + dc) % 2
            start = pl.multiple_of(place * own, 16)
            out[first + i * own : first + (i + 1) * own] = scratch[pl.ds(start, own), :]
    rows = basis.shape[0]
    for i in range(basis.shape[1] // tok):
        for out, first in ((near_other, 8 * own), (far, 16 * own)):
            out[first + i * rows : first + (i + 1) * rows] = basis[:, i * tok : (i + 1) * tok]


def project(steps, at, act, *refs):
    *held, total, last = refs
    z, yh, c = at[0], at[1], at[2]
    rows = held[0].shape[0] // 2

    def columns(dz, dyh, dc):
        place = (((z + dz) % 8) * 2 + (yh + dyh) % 2) * 2 + (c + dc) % 2
        return act[:, pl.ds(pl.multiple_of(place * rows, rows), rows)]

    result = jnp.zeros(total.shape, F32)
    for i, block in enumerate(held):
        for j, dz in enumerate(steps[i // 2]):
            for dyh in range(2):
                start = (2 * j + dyh) * rows
                result += jnp.dot(
                    columns(dz, dyh, i % 2), block[start : start + rows], preferred_element_type=F32
                )
    total[...] = result
    for i in range(4):
        last[:, i * rows : (i + 1) * rows] = columns(4, i % 2, i // 2)


def partial_sums(lo, at, near_own, far, crossed, *refs):
    *mats, out = refs
    wide = mats[0].shape[1]
    rows = slice(lo, lo + out.shape[0])
    second = slice(crossed.shape[0] // 2 + lo, crossed.shape[0] // 2 + rows.stop)
    grads = (near_own[rows], far[rows], crossed[rows], crossed[second])
    for n in range(2):
        result = jnp.dot(grads[0], mats[n][...], preferred_element_type=F32)
        for k in (1, 2, 3):
            result += jnp.dot(grads[k], mats[2 * k + n][...], preferred_element_type=F32)
        out[:, n * wide : (n + 1) * wide] = result.astype(out.dtype)


def adam(count, at, here, up, down, first, second, *outs):
    own, cols = first.shape[0], first.shape[1] // 8
    for i in range(8):
        place = at[3 + i]
        there = pl.ds(pl.multiple_of(place * cols, cols), cols)
        here_cols = slice(i * cols, (i + 1) * cols)
        total = here[-own:, here_cols]
        for part in (up, down):
            total += part[:, here_cols].astype(F32)
        low_grad = total / count
        one = 0.9 * first[:, there] + 0.1 * low_grad
        two = 0.999 * second[:, there] + 0.001 * low_grad * low_grad
        if len(outs) == 2:
            outs[0][:, there], outs[1][:, there] = one, two
        else:
            correct_one = 1.0 - 0.9**STEP
            correct_two = 1.0 - 0.999**STEP
            outs[0][:, there] = (
                one / correct_one / (jnp.sqrt(two / correct_two) + 1e-08)
            ).astype(BF16)


def make(own, n, at, basis, far, crossed, *refs):
    blocks, (mine, other, beyond) = refs[:n], refs[-3:]
    rows, rank = basis.shape
    wide = far.shape[1]
    held = jnp.concatenate([block[...] for block in blocks])
    mine[...] = lax.dot_general(held, basis[...], TURN, preferred_element_type=F32).astype(BF16)
    for mat, first, out, cols in (
        (crossed, 8 * own, other, slice(0, rows)),
        (far, 16 * own, beyond, slice(0, rows)),
        (crossed, 8 * own + crossed.shape[0] // 2, beyond, slice(rows, 2 * rows)),
    ):
        result = jnp.zeros((held.shape[0], rows), F32)
        for i in range(rank // wide):
            part = mat[first + i * rows : first + (i + 1) * rows]
            result += lax.dot_general(
                held[:, i * wide : (i + 1) * wide], part, TURN, preferred_element_type=F32
            )
        out[:, cols] = result.astype(BF16)


def make_first(own, count, at, basis, far, crossed, *refs):
    blocks, moments, made, kept = refs[:3], refs[3:8], refs[8:11], refs[11:]
    make(own, 3, at, basis, far, crossed, *blocks, *made)
    adam(count, at, *moments, *kept)


def place_update(at, *refs):
    near, far, others, (out, scratch) = refs[:4], refs[4:8], refs[8:10], refs[10:12]
    turned, sems = refs[12:]
    z, yh, c = at[0], at[1], at[2]
    rows = out.shape[0]
    own = out.shape[1] // 32
    begin = [0, 0]
    for g, dzs in enumerate(GROUPS):
        for dyh, made in enumerate((near[g], far[g])):
            for i, dz in enumerate(dzs):
                for dc in range(2):
                    place = ((z + dz) % 8) * 4 + ((yh + dyh) % 2) * 2 + (c + dc) % 2
                    there = pl.ds(pl.multiple_of(place * own, 16), own)
                    if dc == 0:
                        scratch[there, :] = made[i * own : (i + 1) * own, :rows]
                    else:
                        start = begin[g // 2] + i * own
                        scratch[there, :] = others[g // 2][start : start + own]
            begin[g // 2] += len(dzs) * own
    w = out.shape[1] // 4
    copies = []
    for i in range(4):
        cols = slice(i * w, (i + 1) * w)
        turned[:, cols] = scratch[cols, :].T
        copies.append(pltpu.make_async_copy(turned.at[:, cols], out.at[:, cols], sems.at[i]))
        copies[-1].start()
    for copy in copies:
        copy.wait()


def shards(activations, out_grad, basis, first_moment, second_moment):
    tok, width = activations.shape
    ff = out_grad.shape[1]
    rows, rank = basis.shape
    own = ff // 32
    cols = rank // 8
    half = own // 32 * 16
    z, yh, c, yl, x = (lax.axis_index(a) for a in AXES)
    by_distance = [((yl + i) % 2) * 4 + (x + j) % 4 for i in range(2) for j in range(4)]
    at = jnp.stack([z, yh, c] + by_distance).astype(jnp.int32)

    mine = lax.dynamic_slice_in_dim(basis, (yl * 4 + x) * cols, cols, 1)
    near_own, near_other, far = on_core(
        turn_grad,
        tuple(
            jax.ShapeDtypeStruct((n, tok), BF16)
            for n in (8 * own, 8 * own + rows * rank // tok, 16 * own + rows * rank // tok)
        ),
        at, out_grad, basis,
        scratch=[pltpu.VMEM((ff, tok), BF16)],
    )
    pair = jnp.concatenate([mine, swap(mine, "yh")])
    pair, near_own, near_other, far = tie(pair, near_own, near_other, far)
    far = swap(far, "yh")
    up, down = pair, pair
    held = [pair, swap(pair, "c")]
    for _ in range(3):
        up, down = shift(up, "z", 1), shift(down, "z", -1)
        both = jnp.concatenate([down, up])
        held += [both, swap(both, "c")]
    total, act = on_core(
        functools.partial(project, ((0,), (1, 7), (2, 6), (3, 5))),
        (jax.ShapeDtypeStruct((tok, cols), F32), jax.ShapeDtypeStruct((tok, 4 * rows), BF16)),
        at, activations, *held,
        flops=2 * tok * width * cols,
    )
    last = jnp.concatenate([shift(up[:rows], "z", 1), shift(down[rows:], "z", -1)])
    last = jnp.concatenate([last, swap(last, "c")])
    total, act = tie(total, act)
    projected = (total + jnp.dot(act, last, preferred_element_type=F32)).astype(BF16)

    line = jnp.concatenate([projected] + [shift(projected, "x", -d) for d in (1, 2, 3)], 1)
    line, far = tie(line, far)
    crossed = swap(jnp.concatenate([near_other, far[8 * own :]]), "c")
    pieces = [line, swap(line, "yl"), swap(line, "yh"), swap(line, "yh", "yl")]
    others = (far, crossed)
    mats = (*pieces, *[swap(piece, "c") for piece in pieces])

    def partial(lo, hi, dtype):
        return on_core(
            functools.partial(partial_sums, lo * own),
            jax.ShapeDtypeStruct(((hi - lo) * own, rank), dtype),
            at, near_own, *others, *mats,
            flops=2 * (hi - lo) * own * 4 * tok * rank,
        )

    first = partial(0, 1, BF16)
    up, down = shift(first[:half], "z", 1), shift(first[half:], "z", -1)
    rest = partial(1, 8, F32)
    three, five = rest[:own], rest[own : 2 * own]
    up = shift(jnp.concatenate([three[:half] + up, three[half:]]).astype(BF16), "z", 1)
    down = shift(jnp.concatenate([five[:half], five[half:] + down]).astype(BF16), "z", -1)
    for i in (2, 4):
        up = shift((rest[i * own : (i + 1) * own] + up).astype(BF16), "z", 1)
        down = shift((rest[(i + 1) * own : (i + 2) * own] + down).astype(BF16), "z", -1)
    state = jax.ShapeDtypeStruct((own, rank), F32)
    moments = (rest, up, down, first_moment, second_moment)
    normalized = on_core(
        functools.partial(adam, tok * 32), jax.ShapeDtypeStruct((own, rank), BF16), at, *moments
    )

    def made(blocks, kernel, *moments):
        n = sum(block.shape[0] for block in blocks)
        near, other, beyond, *kept = on_core(
            kernel,
            [jax.ShapeDtypeStruct((n, i * rows), BF16) for i in (1, 1, 2)] + [state] * (len(moments) and 2),
            at, basis, *others, *blocks, *moments,
            flops=2 * n * 4 * rows * rank,
        )
        return (near, other, swap(beyond, "yh")), kept

    up, down = shift(normalized, "z", 1), shift(normalized, "z", -1)
    first = functools.partial(make_first, own, tok * 32)
    group, (new_first, new_second) = made((normalized, down, up), first, *moments)
    groups = [group]
    for _ in range(2):
        up, down = shift(up, "z", 1), shift(down, "z", -1)
        groups.append(made((down, up), functools.partial(make, own, 2))[0])
    ends = (shift(up[:half], "z", 1), shift(down[half:], "z", -1))
    groups.append(made(ends, functools.partial(make, own, 2))[0])
    crossed = [
        swap(jnp.concatenate([p for g in some for p in (groups[g][1], groups[g][2][:, rows:])]), "c")
        for some in ((0, 1), (2, 3))
    ]
    made_up = (*[group[0] for group in groups], *[group[2] for group in groups], *crossed)
    update = pl.pallas_call(
        place_update,
        out_shape=jax.ShapeDtypeStruct((rows, ff), BF16),
        in_specs=[pl.BlockSpec(memory_space=pltpu.SMEM)]
        + [pl.BlockSpec(memory_space=pltpu.VMEM)] * len(made_up),
        out_specs=pl.BlockSpec(memory_space=pl.ANY),
        scratch_shapes=[
            pltpu.VMEM((ff, rows), BF16),
            pltpu.VMEM((rows, ff), BF16),
            pltpu.SemaphoreType.DMA((4,)),
        ],
        cost_estimate=pl.CostEstimate(flops=0, bytes_accessed=4 * rows * ff, transcendentals=0),
        compiler_params=pltpu.CompilerParams(vmem_limit_bytes=40 * 2**20),
    )(at, *made_up)
    return (update, new_first, new_second)


def solution(mesh):
    grid = Mesh(mesh.devices.reshape(tuple(AXES.values())), tuple(AXES))
    placed = (P(DP, None), P(DP, MP), P(DP, None), P(MP + DP, None), P(MP + DP, None))
    return jax.shard_map(
        shards,
        mesh=grid,
        in_specs=placed,
        out_specs=(P(DP, MP), P(MP + DP, None), P(MP + DP, None)),
        check_vma=False,
    )
```

```python
import functools

import jax
import jax.numpy as jnp
from jax import lax
from jax.experimental import pallas as pl
from jax.experimental.pallas import tpu as pltpu
from jax.sharding import Mesh, PartitionSpec as P

STEP = 10
AXES = {"z": 8, "yh": 2, "c": 2, "yl": 2, "x": 4}
DP = ("z", "yh", "c")
MP = ("yl", "x")
F32 = jnp.float32
BF16 = jnp.bfloat16
TURN = (((1,), (1,)), ((), ()))
SUMS = (4, 3, 5, 2, 6, 1, 7, 0)

GROUPS = ((0, 1, 7), (2, 6), (3, 5), (4,))


def shift(value, axis, by):
    n = AXES[axis]
    return lax.ppermute(value, axis, [(i, (i + by) % n) for i in range(n)])


def swap(value, *axes):
    n = 2 ** len(axes)
    return lax.ppermute(value, axes, [(i, n - 1 - i) for i in range(n)])


def tie(*values):
    return lax.optimization_barrier(values)


def on_core(body, out, scalars, *arrays, flops=0, scratch=()):
    size = sum(a.size * a.dtype.itemsize for a in arrays)
    return pl.pallas_call(
        body,
        out_shape=out,
        in_specs=[pl.BlockSpec(memory_space=pltpu.SMEM)]
        + [pl.BlockSpec(memory_space=pltpu.VMEM)] * len(arrays),
        out_specs=jax.tree.map(lambda _: pl.BlockSpec(memory_space=pltpu.VMEM), out),
        scratch_shapes=list(scratch),
        cost_estimate=pl.CostEstimate(flops=flops, bytes_accessed=size, transcendentals=0),
        compiler_params=pltpu.CompilerParams(vmem_limit_bytes=40 * 2**20),
    )(scalars, *arrays)


def turn_grad(at, grad, basis, near_own, near_other, far, scratch):
    z, yh, c = at[0], at[1], at[2]
    tok, ff = grad.shape
    own = ff // 32
    w = ff // 8
    for i in range(8):
        scratch[i * w : (i + 1) * w, :] = grad[:, i * w : (i + 1) * w].T
    for i, dz in enumerate(SUMS):
        for dyh, dc, out, first in ((0, 0, near_own, 0), (0, 1, near_other, 0), (1, 0, far, 0), (1, 1, far, 8 * own)):
            place = ((z + dz) % 8) * 4 + ((yh + dyh) % 2) * 2 + (c + dc) % 2
            start = pl.multiple_of(place * own, 16)
            out[first + i * own : first + (i + 1) * own] = scratch[pl.ds(start, own), :]
    rows = basis.shape[0]
    for i in range(basis.shape[1] // tok):
        for out, first in ((near_other, 8 * own), (far, 16 * own)):
            out[first + i * rows : first + (i + 1) * rows] = basis[:, i * tok : (i + 1) * tok]


def project(steps, at, act, *refs):
    *held, total, last = refs
    z, yh, c = at[0], at[1], at[2]
    rows = held[0].shape[0] // 2

    def columns(dz, dyh, dc):
        place = (((z + dz) % 8) * 2 + (yh + dyh) % 2) * 2 + (c + dc) % 2
        return act[:, pl.ds(pl.multiple_of(place * rows, rows), rows)]

    result = jnp.zeros(total.shape, F32)
    for i, block in enumerate(held):
        for j, dz in enumerate(steps[i // 2]):
            for dyh in range(2):
                start = (2 * j + dyh) * rows
                result += jnp.dot(
                    columns(dz, dyh, i % 2), block[start : start + rows], preferred_element_type=F32
                )
    total[...] = result
    for i in range(4):
        last[:, i * rows : (i + 1) * rows] = columns(4, i % 2, i // 2)


def partial_sums(lo, at, near_own, far, crossed, *refs):
    *mats, out = refs
    wide = mats[0].shape[1]
    rows = slice(lo, lo + out.shape[0])
    second = slice(crossed.shape[0] // 2 + lo, crossed.shape[0] // 2 + rows.stop)
    grads = (near_own[rows], far[rows], crossed[rows], crossed[second])
    for n in range(2):
        result = jnp.dot(grads[0], mats[n][...], preferred_element_type=F32)
        for k in (1, 2, 3):
            result += jnp.dot(grads[k], mats[2 * k + n][...], preferred_element_type=F32)
        out[:, n * wide : (n + 1) * wide] = result.astype(out.dtype)


def adam(count, at, here, up, down, first, second, *outs):
    own, cols = first.shape[0], first.shape[1] // 8
    for i in range(8):
        place = at[3 + i]
        there = pl.ds(pl.multiple_of(place * cols, cols), cols)
        here_cols = slice(i * cols, (i + 1) * cols)
        total = here[-own:, here_cols]
        for part in (up, down):
            total += part[:, here_cols].astype(F32)
        low_grad = total / count
        one = 0.9 * first[:, there] + 0.1 * low_grad
        two = 0.999 * second[:, there] + 0.001 * low_grad * low_grad
        if len(outs) == 2:
            outs[0][:, there], outs[1][:, there] = one, two
        else:
            correct_one = 1.0 - 0.9**STEP
            correct_two = 1.0 - 0.999**STEP
            outs[0][:, there] = (
                one / correct_one / (jnp.sqrt(two / correct_two) + 1e-08)
            ).astype(BF16)


def make(own, n, at, basis, far, crossed, *refs):
    blocks, (mine, other, beyond) = refs[:n], refs[-3:]
    rows, rank = basis.shape
    wide = far.shape[1]
    held = jnp.concatenate([block[...] for block in blocks])
    mine[...] = lax.dot_general(held, basis[...], TURN, preferred_element_type=F32).astype(BF16)
    for mat, first, out, cols in (
        (crossed, 8 * own, other, slice(0, rows)),
        (far, 16 * own, beyond, slice(0, rows)),
        (crossed, 8 * own + crossed.shape[0] // 2, beyond, slice(rows, 2 * rows)),
    ):
        result = jnp.zeros((held.shape[0], rows), F32)
        for i in range(rank // wide):
            part = mat[first + i * rows : first + (i + 1) * rows]
            result += lax.dot_general(
                held[:, i * wide : (i + 1) * wide], part, TURN, preferred_element_type=F32
            )
        out[:, cols] = result.astype(BF16)


def make_first(own, count, at, basis, far, crossed, *refs):
    blocks, moments, made, kept = refs[:3], refs[3:8], refs[8:11], refs[11:]
    make(own, 3, at, basis, far, crossed, *blocks, *made)
    adam(count, at, *moments, *kept)


def place_update(at, *refs):
    near, far, others, (out, scratch) = refs[:4], refs[4:8], refs[8:10], refs[10:12]
    turned, sems = refs[12:]
    z, yh, c = at[0], at[1], at[2]
    rows = out.shape[0]
    own = out.shape[1] // 32
    begin = [0, 0]
    for g, dzs in enumerate(GROUPS):
        for dyh, made in enumerate((near[g], far[g])):
            for i, dz in enumerate(dzs):
                for dc in range(2):
                    place = ((z + dz) % 8) * 4 + ((yh + dyh) % 2) * 2 + (c + dc) % 2
                    there = pl.ds(pl.multiple_of(place * own, 16), own)
                    if dc == 0:
                        scratch[there, :] = made[i * own : (i + 1) * own, :rows]
                    else:
                        start = begin[g // 2] + i * own
                        scratch[there, :] = others[g // 2][start : start + own]
            begin[g // 2] += len(dzs) * own
    w = out.shape[1] // 4
    copies = []
    for i in range(4):
        cols = slice(i * w, (i + 1) * w)
        turned[:, cols] = scratch[cols, :].T
        copies.append(pltpu.make_async_copy(turned.at[:, cols], out.at[:, cols], sems.at[i]))
        copies[-1].start()
    for copy in copies:
        copy.wait()


def shards(activations, out_grad, basis, first_moment, second_moment):
    tok, width = activations.shape
    ff = out_grad.shape[1]
    rows, rank = basis.shape
    own = ff // 32
    cols = rank // 8
    half = own // 32 * 16
    z, yh, c, yl, x = (lax.axis_index(a) for a in AXES)
    by_distance = [((yl + i) % 2) * 4 + (x + j) % 4 for i in range(2) for j in range(4)]
    at = jnp.stack([z, yh, c] + by_distance).astype(jnp.int32)

    mine = lax.dynamic_slice_in_dim(basis, (yl * 4 + x) * cols, cols, 1)
    near_own, near_other, far = on_core(
        turn_grad,
        tuple(
            jax.ShapeDtypeStruct((n, tok), BF16)
            for n in (8 * own, 8 * own + rows * rank // tok, 16 * own + rows * rank // tok)
        ),
        at, out_grad, basis,
        scratch=[pltpu.VMEM((ff, tok), BF16)],
    )
    pair = jnp.concatenate([mine, swap(mine, "yh")])
    pair, near_own, near_other, far = tie(pair, near_own, near_other, far)
    far = swap(far, "yh")
    up, down = pair, pair
    held = [pair, swap(pair, "c")]
    for _ in range(3):
        up, down = shift(up, "z", 1), shift(down, "z", -1)
        both = jnp.concatenate([down, up])
        held += [both, swap(both, "c")]
    total, act = on_core(
        functools.partial(project, ((0,), (1, 7), (2, 6), (3, 5))),
        (jax.ShapeDtypeStruct((tok, cols), F32), jax.ShapeDtypeStruct((tok, 4 * rows), BF16)),
        at, activations, *held,
        flops=2 * tok * width * cols,
    )
    last = jnp.concatenate([shift(up[:rows], "z", 1), shift(down[rows:], "z", -1)])
    last = jnp.concatenate([last, swap(last, "c")])
    total, act = tie(total, act)
    projected = (total + jnp.dot(act, last, preferred_element_type=F32)).astype(BF16)

    line = jnp.concatenate([projected] + [shift(projected, "x", -d) for d in (1, 2, 3)], 1)
    line, far = tie(line, far)
    crossed = swap(jnp.concatenate([near_other, far[8 * own :]]), "c")
    pieces = [line, swap(line, "yl"), swap(line, "yh"), swap(line, "yh", "yl")]
    others = (far, crossed)
    mats = (*pieces, *[swap(piece, "c") for piece in pieces])

    def partial(lo, hi, dtype):
        return on_core(
            functools.partial(partial_sums, lo * own),
            jax.ShapeDtypeStruct(((hi - lo) * own, rank), dtype),
            at, near_own, *others, *mats,
            flops=2 * (hi - lo) * own * 4 * tok * rank,
        )

    first = partial(0, 1, BF16)
    up, down = shift(first[:half], "z", 1), shift(first[half:], "z", -1)
    next_two = partial(1, 3, F32)
    later = partial(3, 5, F32)
    rest = partial(5, 8, F32)
    three, five = next_two[:own], next_two[own:]
    up = shift(jnp.concatenate([three[:half] + up, three[half:]]).astype(BF16), "z", 1)
    down = shift(jnp.concatenate([five[:half], five[half:] + down]).astype(BF16), "z", -1)
    for part in (later, rest):
        up = shift((part[:own] + up).astype(BF16), "z", 1)
        down = shift((part[own : 2 * own] + down).astype(BF16), "z", -1)
    state = jax.ShapeDtypeStruct((own, rank), F32)
    moments = (rest, up, down, first_moment, second_moment)
    normalized = on_core(
        functools.partial(adam, tok * 32), jax.ShapeDtypeStruct((own, rank), BF16), at, *moments
    )

    def made(blocks, kernel, *moments):
        n = sum(block.shape[0] for block in blocks)
        near, other, beyond, *kept = on_core(
            kernel,
            [jax.ShapeDtypeStruct((n, i * rows), BF16) for i in (1, 1, 2)] + [state] * (len(moments) and 2),
            at, basis, *others, *blocks, *moments,
            flops=2 * n * 4 * rows * rank,
        )
        return (near, other, swap(beyond, "yh")), kept

    up, down = shift(normalized, "z", 1), shift(normalized, "z", -1)
    first = functools.partial(make_first, own, tok * 32)
    group, (new_first, new_second) = made((normalized, down, up), first, *moments)
    groups = [group]
    for _ in range(2):
        up, down = shift(up, "z", 1), shift(down, "z", -1)
        groups.append(made((down, up), functools.partial(make, own, 2))[0])
    ends = (shift(up[:half], "z", 1), shift(down[half:], "z", -1))
    groups.append(made(ends, functools.partial(make, own, 2))[0])
    crossed = [
        swap(jnp.concatenate([p for g in some for p in (groups[g][1], groups[g][2][:, rows:])]), "c")
        for some in ((0, 1), (2, 3))
    ]
    made_up = (*[group[0] for group in groups], *[group[2] for group in groups], *crossed)
    update = pl.pallas_call(
        place_update,
        out_shape=jax.ShapeDtypeStruct((rows, ff), BF16),
        in_specs=[pl.BlockSpec(memory_space=pltpu.SMEM)]
        + [pl.BlockSpec(memory_space=pltpu.VMEM)] * len(made_up),
        out_specs=pl.BlockSpec(memory_space=pl.ANY),
        scratch_shapes=[
            pltpu.VMEM((ff, rows), BF16),
            pltpu.VMEM((rows, ff), BF16),
            pltpu.SemaphoreType.DMA((4,)),
        ],
        cost_estimate=pl.CostEstimate(flops=0, bytes_accessed=4 * rows * ff, transcendentals=0),
        compiler_params=pltpu.CompilerParams(vmem_limit_bytes=40 * 2**20),
    )(at, *made_up)
    return (update, new_first, new_second)


def solution(mesh):
    grid = Mesh(mesh.devices.reshape(tuple(AXES.values())), tuple(AXES))
    placed = (P(DP, None), P(DP, MP), P(DP, None), P(MP + DP, None), P(MP + DP, None))
    return jax.shard_map(
        shards,
        mesh=grid,
        in_specs=placed,
        out_specs=(P(DP, MP), P(MP + DP, None), P(MP + DP, None)),
        check_vma=False,
    )
```

```python
import functools

import jax
import jax.numpy as jnp
from jax import lax
from jax.experimental import pallas as pl
from jax.experimental.pallas import tpu as pltpu
from jax.sharding import Mesh, PartitionSpec as P

STEP = 10
AXES = {"z": 8, "yh": 2, "c": 2, "yl": 2, "x": 4}
DP = ("z", "yh", "c")
MP = ("yl", "x")
F32 = jnp.float32
BF16 = jnp.bfloat16
TURN = (((1,), (1,)), ((), ()))
SUMS = (4, 3, 5, 2, 6, 1, 7, 0)

GROUPS = ((0, 1, 7), (2, 6), (3, 5), (4,))


def shift(value, axis, by):
    n = AXES[axis]
    return lax.ppermute(value, axis, [(i, (i + by) % n) for i in range(n)])


def swap(value, *axes):
    n = 2 ** len(axes)
    return lax.ppermute(value, axes, [(i, n - 1 - i) for i in range(n)])


def tie(*values):
    return lax.optimization_barrier(values)


def on_core(body, out, scalars, *arrays, flops=0, scratch=()):
    size = sum(a.size * a.dtype.itemsize for a in arrays)
    return pl.pallas_call(
        body,
        out_shape=out,
        in_specs=[pl.BlockSpec(memory_space=pltpu.SMEM)]
        + [pl.BlockSpec(memory_space=pltpu.VMEM)] * len(arrays),
        out_specs=jax.tree.map(lambda _: pl.BlockSpec(memory_space=pltpu.VMEM), out),
        scratch_shapes=list(scratch),
        cost_estimate=pl.CostEstimate(flops=flops, bytes_accessed=size, transcendentals=0),
        compiler_params=pltpu.CompilerParams(vmem_limit_bytes=40 * 2**20),
    )(scalars, *arrays)


def turn_grad(at, grad, basis, near_own, near_other, far, scratch):
    z, yh, c = at[0], at[1], at[2]
    tok, ff = grad.shape
    own = ff // 32
    w = ff // 8
    for i in range(8):
        scratch[i * w : (i + 1) * w, :] = grad[:, i * w : (i + 1) * w].T
    for i, dz in enumerate(SUMS):
        for dyh, dc, out, first in ((0, 0, near_own, 0), (0, 1, near_other, 0), (1, 0, far, 0), (1, 1, far, 8 * own)):
            place = ((z + dz) % 8) * 4 + ((yh + dyh) % 2) * 2 + (c + dc) % 2
            start = pl.multiple_of(place * own, 16)
            out[first + i * own : first + (i + 1) * own] = scratch[pl.ds(start, own), :]
    rows = basis.shape[0]
    for i in range(basis.shape[1] // tok):
        for out, first in ((near_other, 8 * own), (far, 16 * own)):
            out[first + i * rows : first + (i + 1) * rows] = basis[:, i * tok : (i + 1) * tok]


def project(steps, at, act, *refs):
    *held, total, last = refs
    z, yh, c = at[0], at[1], at[2]
    rows = held[0].shape[0] // 2

    def columns(dz, dyh, dc):
        place = (((z + dz) % 8) * 2 + (yh + dyh) % 2) * 2 + (c + dc) % 2
        return act[:, pl.ds(pl.multiple_of(place * rows, rows), rows)]

    result = jnp.zeros(total.shape, F32)
    for i, block in enumerate(held):
        for j, dz in enumerate(steps[i // 2]):
            for dyh in range(2):
                start = (2 * j + dyh) * rows
                result += jnp.dot(
                    columns(dz, dyh, i % 2), block[start : start + rows], preferred_element_type=F32
                )
    total[...] = result
    for i in range(4):
        last[:, i * rows : (i + 1) * rows] = columns(4, i % 2, i // 2)


def partial_sums(lo, at, near_own, far, crossed, *refs):
    *mats, out = refs
    wide = mats[0].shape[1]
    rows = slice(lo, lo + out.shape[0])
    second = slice(crossed.shape[0] // 2 + lo, crossed.shape[0] // 2 + rows.stop)
    grads = (near_own[rows], far[rows], crossed[rows], crossed[second])
    for n in range(2):
        result = jnp.dot(grads[0], mats[n][...], preferred_element_type=F32)
        for k in (1, 2, 3):
            result += jnp.dot(grads[k], mats[2 * k + n][...], preferred_element_type=F32)
        out[:, n * wide : (n + 1) * wide] = result.astype(out.dtype)


def adam(count, at, here, up, down, first, second, *outs):
    own, cols = first.shape[0], first.shape[1] // 8
    for i in range(8):
        place = at[3 + i]
        there = pl.ds(pl.multiple_of(place * cols, cols), cols)
        here_cols = slice(i * cols, (i + 1) * cols)
        total = here[-own:, here_cols]
        for part in (up, down):
            total += part[:, here_cols].astype(F32)
        low_grad = total / count
        one = 0.9 * first[:, there] + 0.1 * low_grad
        two = 0.999 * second[:, there] + 0.001 * low_grad * low_grad
        if len(outs) == 2:
            outs[0][:, there], outs[1][:, there] = one, two
        else:
            correct_one = 1.0 - 0.9**STEP
            correct_two = 1.0 - 0.999**STEP
            outs[0][:, there] = (
                one / correct_one / (jnp.sqrt(two / correct_two) + 1e-08)
            ).astype(BF16)


def in_blocks(held, mat, first, rows):
    wide = mat.shape[1]
    result = jnp.zeros((held.shape[0], rows), F32)
    for i in range(held.shape[1] // wide):
        part = mat[first + i * rows : first + (i + 1) * rows]
        result += lax.dot_general(
            held[:, i * wide : (i + 1) * wide], part, TURN, preferred_element_type=F32
        )
    return result.astype(BF16)


def make_far(own, at, far, crossed, *refs):
    *blocks, out = refs
    rows = out.shape[1] // 2
    held = jnp.concatenate([block[...] for block in blocks])
    out[:, :rows] = in_blocks(held, far, 16 * own, rows)
    out[:, rows:] = in_blocks(held, crossed, 8 * own + crossed.shape[0] // 2, rows)


def make_near(own, n, count, at, basis, crossed, *refs):
    blocks, refs = refs[:n], refs[n:]
    if len(refs) == 9:
        adam(count, at, *refs[:5], *refs[7:])
        refs = refs[5:7]
    mine, other = refs
    held = jnp.concatenate([block[...] for block in blocks])
    mine[...] = lax.dot_general(held, basis[...], TURN, preferred_element_type=F32).astype(BF16)
    other[...] = in_blocks(held, crossed, 8 * own, basis.shape[0])


def place_update(at, *refs):
    near, far, others, (out, scratch) = refs[:4], refs[4:8], refs[8:10], refs[10:12]
    turned, sems = refs[12:]
    z, yh, c = at[0], at[1], at[2]
    rows = out.shape[0]
    own = out.shape[1] // 32
    begin = [0, 0]
    for g, dzs in enumerate(GROUPS):
        for dyh, made in enumerate((near[g], far[g])):
            for i, dz in enumerate(dzs):
                for dc in range(2):
                    place = ((z + dz) % 8) * 4 + ((yh + dyh) % 2) * 2 + (c + dc) % 2
                    there = pl.ds(pl.multiple_of(place * own, 16), own)
                    if dc == 0:
                        scratch[there, :] = made[i * own : (i + 1) * own, :rows]
                    else:
                        start = begin[g // 2] + i * own
                        scratch[there, :] = others[g // 2][start : start + own]
            begin[g // 2] += len(dzs) * own
    w = out.shape[1] // 4
    copies = []
    for i in range(4):
        cols = slice(i * w, (i + 1) * w)
        turned[:, cols] = scratch[cols, :].T
        copies.append(pltpu.make_async_copy(turned.at[:, cols], out.at[:, cols], sems.at[i]))
        copies[-1].start()
    for copy in copies:
        copy.wait()


def shards(activations, out_grad, basis, first_moment, second_moment):
    tok, width = activations.shape
    ff = out_grad.shape[1]
    rows, rank = basis.shape
    own = ff // 32
    cols = rank // 8
    half = own // 32 * 16
    z, yh, c, yl, x = (lax.axis_index(a) for a in AXES)
    by_distance = [((yl + i) % 2) * 4 + (x + j) % 4 for i in range(2) for j in range(4)]
    at = jnp.stack([z, yh, c] + by_distance).astype(jnp.int32)

    mine = lax.dynamic_slice_in_dim(basis, (yl * 4 + x) * cols, cols, 1)
    near_own, near_other, far = on_core(
        turn_grad,
        tuple(
            jax.ShapeDtypeStruct((n, tok), BF16)
            for n in (8 * own, 8 * own + rows * rank // tok, 16 * own + rows * rank // tok)
        ),
        at, out_grad, basis,
        scratch=[pltpu.VMEM((ff, tok), BF16)],
    )
    pair = jnp.concatenate([mine, swap(mine, "yh")])
    pair, near_own, near_other, far = tie(pair, near_own, near_other, far)
    far = swap(far, "yh")
    up, down = pair, pair
    held = [pair, swap(pair, "c")]
    for _ in range(3):
        up, down = shift(up, "z", 1), shift(down, "z", -1)
        both = jnp.concatenate([down, up])
        held += [both, swap(both, "c")]
    total, act = on_core(
        functools.partial(project, ((0,), (1, 7), (2, 6), (3, 5))),
        (jax.ShapeDtypeStruct((tok, cols), F32), jax.ShapeDtypeStruct((tok, 4 * rows), BF16)),
        at, activations, *held,
        flops=2 * tok * width * cols,
    )
    last = jnp.concatenate([shift(up[:rows], "z", 1), shift(down[rows:], "z", -1)])
    last = jnp.concatenate([last, swap(last, "c")])
    total, act = tie(total, act)
    projected = (total + jnp.dot(act, last, preferred_element_type=F32)).astype(BF16)

    line = jnp.concatenate([projected] + [shift(projected, "x", -d) for d in (1, 2, 3)], 1)
    line, far = tie(line, far)
    crossed = swap(jnp.concatenate([near_other, far[8 * own :]]), "c")
    pieces = [line, swap(line, "yl"), swap(line, "yh"), swap(line, "yh", "yl")]
    others = (far, crossed)
    mats = (*pieces, *[swap(piece, "c") for piece in pieces])

    def partial(lo, hi, dtype):
        return on_core(
            functools.partial(partial_sums, lo * own),
            jax.ShapeDtypeStruct(((hi - lo) * own, rank), dtype),
            at, near_own, *others, *mats,
            flops=2 * (hi - lo) * own * 4 * tok * rank,
        )

    first = partial(0, 1, BF16)
    up, down = shift(first[:half], "z", 1), shift(first[half:], "z", -1)
    next_two = partial(1, 3, F32)
    later = partial(3, 5, F32)
    rest = partial(5, 8, F32)
    three, five = next_two[:own], next_two[own:]
    up = shift(jnp.concatenate([three[:half] + up, three[half:]]).astype(BF16), "z", 1)
    down = shift(jnp.concatenate([five[:half], five[half:] + down]).astype(BF16), "z", -1)
    for part in (later, rest):
        up = shift((part[:own] + up).astype(BF16), "z", 1)
        down = shift((part[own : 2 * own] + down).astype(BF16), "z", -1)
    state = jax.ShapeDtypeStruct((own, rank), F32)
    moments = (rest, up, down, first_moment, second_moment)
    normalized = on_core(
        functools.partial(adam, tok * 32), jax.ShapeDtypeStruct((own, rank), BF16), at, *moments
    )

    def made(blocks, *moments):
        n = sum(block.shape[0] for block in blocks)
        beyond = on_core(
            functools.partial(make_far, own),
            jax.ShapeDtypeStruct((n, 2 * rows), BF16),
            at, *others, *blocks,
            flops=2 * n * 2 * rows * rank,
        )
        beyond = swap(beyond, "yh")
        near, other, *kept = on_core(
            functools.partial(make_near, own, len(blocks), tok * 32),
            [jax.ShapeDtypeStruct((n, rows), BF16)] * 2 + [state] * (len(moments) and 2),
            at, basis, others[1], *blocks, *moments,
            flops=2 * n * 2 * rows * rank,
        )
        return (near, other, beyond), kept

    up, down = shift(normalized, "z", 1), shift(normalized, "z", -1)
    group, (new_first, new_second) = made((normalized, down, up), *moments)
    groups = [group]
    for _ in range(2):
        up, down = shift(up, "z", 1), shift(down, "z", -1)
        groups.append(made((down, up))[0])
    ends = (shift(up[:half], "z", 1), shift(down[half:], "z", -1))
    groups.append(made(ends)[0])
    crossed = [
        swap(jnp.concatenate([p for g in some for p in (groups[g][1], groups[g][2][:, rows:])]), "c")
        for some in ((0, 1), (2, 3))
    ]
    made_up = (*[group[0] for group in groups], *[group[2] for group in groups], *crossed)
    update = pl.pallas_call(
        place_update,
        out_shape=jax.ShapeDtypeStruct((rows, ff), BF16),
        in_specs=[pl.BlockSpec(memory_space=pltpu.SMEM)]
        + [pl.BlockSpec(memory_space=pltpu.VMEM)] * len(made_up),
        out_specs=pl.BlockSpec(memory_space=pl.ANY),
        scratch_shapes=[
            pltpu.VMEM((ff, rows), BF16),
            pltpu.VMEM((rows, ff), BF16),
            pltpu.SemaphoreType.DMA((4,)),
        ],
        cost_estimate=pl.CostEstimate(flops=0, bytes_accessed=4 * rows * ff, transcendentals=0),
        compiler_params=pltpu.CompilerParams(vmem_limit_bytes=40 * 2**20),
    )(at, *made_up)
    return (update, new_first, new_second)


def solution(mesh):
    grid = Mesh(mesh.devices.reshape(tuple(AXES.values())), tuple(AXES))
    placed = (P(DP, None), P(DP, MP), P(DP, None), P(MP + DP, None), P(MP + DP, None))
    return jax.shard_map(
        shards,
        mesh=grid,
        in_specs=placed,
        out_specs=(P(DP, MP), P(MP + DP, None), P(MP + DP, None)),
        check_vma=False,
    )
```
